512 devices in a mesh: chan: 32 (over z, y_hi), win: 16 (over y_lo, x, core).
Axes of the slice: x: 4, y: 4 (y_hi: 2, y_lo: 2; y = y_hi * 2 + y_lo), z: 16, core: 2. Of those that a mesh axis runs over, the one named last changes fastest.
Arguments:
- spectra: bfloat16 [32, 10240, 2, 512], P('win', 'chan')
- counts: int32 [32], P('chan'), may hold values from 160 to 320, as said below
- partner: int32 [1, 32], replicated, may hold values from 0 to 31, as said below
Outputs:
- corr: float32 [32, 1, 16, 160, 320], P('chan', None, None, 'win')
The draws below stay inside these ranges and needn't reach their ends.
Inputs may be any that keep to these rules, and one draw needn't show every extreme that they name: `counts`: every block has at least 160 live channels and some block has all 320. partner[q, b] = b XOR t_q for distinct nonzero round numbers t_q, so every round pairs the blocks among themselves.
All inputs are finite; a program needn't handle non-finite values.
Results may differ from the reference program's by a relative error of at most 0.0049.
Values may be sent and summed in bfloat16 or wider, within the bound.
A program may use at most 64 MiB of HBM per device.

```python
import math
import jax
import jax.numpy as jnp
from jax import lax

CB = 320
FREQS = 512
LAGS = 16
SRC = 160
ROUNDS = 1
WINDOWS = 32
BLOCKS = 32
CHANNELS = 10240


def draw_spectra(key, part):
    key = jax.random.fold_in(key, 11)
    first, second = jax.random.split(key)
    noise = jax.random.normal(first, (WINDOWS, CHANNELS, 2, FREQS), jnp.float32)
    levels = jnp.exp(jax.random.uniform(second, (WINDOWS, CHANNELS, 1, 1), jnp.float32, 0.0, math.log(10.0)))
    return (noise * levels).astype(jnp.bfloat16)


def draw_counts(key, part):
    key = jax.random.fold_in(key, 23)
    first, second = jax.random.split(key)
    drawn = jax.random.randint(first, (BLOCKS,), CB // 2, CB + 1)
    full = jax.random.randint(second, (), 0, BLOCKS)
    return jnp.where(jnp.arange(BLOCKS) == full, CB, drawn).astype(jnp.int32)


def draw_partner(key, part):
    key = jax.random.fold_in(key, 37)
    order = jax.random.permutation(key, BLOCKS - 1) + 1
    picked = order[:ROUNDS].astype(jnp.int32)
    channel_blocks = jnp.arange(BLOCKS, dtype=jnp.int32)
    return jnp.bitwise_xor(channel_blocks[None, :], picked[:, None]).astype(jnp.int32)


def setup_inputs(seed: int = 0) -> dict:
    key_list = jax.random.split(jax.random.key(seed), 4)
    spectra = draw_spectra(jax.random.fold_in(key_list[3], 71), 0)
    counts = draw_counts(jax.random.fold_in(key_list[3], 71), 0)
    partner = draw_partner(jax.random.fold_in(key_list[3], 71), 0)
    return {"spectra": spectra, "counts": counts, "partner": partner}


def spectral_whitening(spectra, counts):
    values = spectra.astype(jnp.float32)
    block_positions = jnp.arange(CHANNELS, dtype=jnp.int32) % CB
    owners = jnp.arange(CHANNELS, dtype=jnp.int32) // CB
    valid = (block_positions < counts[owners]).astype(jnp.float32)
    freq = jnp.arange(FREQS, dtype=jnp.float32)
    taper = 0.75 - 0.25 * jnp.cos(2.0 * math.pi * (freq + 0.5) / FREQS)
    power = lax.optimization_barrier(jnp.mean(values * values, axis=(2, 3)))
    scale = valid[None, :] / jnp.sqrt(power + 1e-05)
    return (values * taper * scale[:, :, None, None]).astype(jnp.bfloat16)

def lag_table():
    freq = jnp.arange(FREQS, dtype=jnp.float32) + FREQS // 4
    delay = jnp.arange(LAGS, dtype=jnp.float32) - LAGS // 2
    phase = 2.0 * math.pi * freq[:, None] * delay[None, :] / (4.0 * FREQS)
    norm = 1.0 / math.sqrt(2.0 * FREQS)
    return jnp.stack([jnp.cos(phase), -jnp.sin(phase)]) * norm

def blended_sources(sources, table):
    src = sources.astype(jnp.float32)
    first = src[:, :, 0][:, :, None, :]
    second = src[:, :, 1][:, :, None, :]
    cos_part = table[0].T[None, None]
    sin_part = table[1].T[None, None]
    real_mix = first * cos_part + second * sin_part
    imag_mix = second * cos_part - first * sin_part
    return jnp.stack([real_mix, imag_mix], axis=3).astype(jnp.bfloat16)

def reference(spectra, counts, partner):
    white = spectral_whitening(spectra, counts).reshape(WINDOWS, BLOCKS, CB, 2, FREQS)
    table = lag_table()
    rounds_out = []
    for step in range(ROUNDS):

        def per_block(block):
            other = partner[step, block]
            receiver_blocks = lax.dynamic_index_in_dim(white, other, 1, keepdims=False)
            mine = lax.dynamic_index_in_dim(white, block, 1, keepdims=False)
            mixed_spectra = blended_sources(mine[:, :SRC], table)
            return jnp.einsum('kidtb,katb->dia', mixed_spectra.astype(jnp.float32), receiver_blocks.astype(jnp.float32))
        rounds_out.append(lax.map(per_block, jnp.arange(BLOCKS, dtype=jnp.int32)))
    return jnp.stack(rounds_out, axis=1) / math.sqrt(WINDOWS)
```

```python
import functools
import math

import jax
import jax.numpy as jnp
from jax import lax
from jax.experimental import pallas as pl
from jax.experimental.pallas import tpu as pltpu
from jax.sharding import PartitionSpec as P

LAGS = 16
SRC = 160
MESH = pl.DeviceIdType.MESH


def whiten_rows(spectra, count):
    values = spectra.astype(jnp.float32)
    wins, block_size, two, freqs = spectra.shape
    valid = (jnp.arange(block_size, dtype=jnp.int32) < count).astype(jnp.float32)
    freq = jnp.arange(freqs, dtype=jnp.float32)
    taper = 0.75 - 0.25 * jnp.cos(2.0 * math.pi * (freq + 0.5) / freqs)
    power = jnp.mean(values * values, axis=(2, 3))
    scale = valid[None, :] / jnp.sqrt(power + 1e-05)
    white = (values * taper * scale[:, :, None, None]).astype(jnp.bfloat16)
    return jnp.swapaxes(white, 0, 1).reshape(block_size, wins * two * freqs)


def lag_table(freqs, lags):
    freq = jnp.arange(freqs, dtype=jnp.float32) + freqs // 4
    delay = jnp.arange(lags, dtype=jnp.float32) - lags // 2
    phase = 2.0 * math.pi * freq[None, :] * delay[:, None] / (4.0 * freqs)
    norm = 1.0 / math.sqrt(2.0 * freqs)
    return jnp.cos(phase) * norm, -jnp.sin(phase) * norm


def correlate_kernel(
    scale, src_ref, rec_ref, cos_ref, sin_ref, out_ref,
    src32, mixed, send1, recv1, send2, recv2, sem_s1, sem_r1, sem_s2, sem_r2,
):
    chan = lax.axis_index("chan")
    win = lax.axis_index("win")
    y, x, core = win // 8, lax.rem(win // 2, 4), lax.rem(win, 2)
    sibling = win + 1 - 2 * core
    per = SRC // 16
    rows = per * LAGS
    freqs = cos_ref.shape[1]
    wins = src_ref.shape[1] // (2 * freqs)

    def place(d):
        return lax.rem(y + d // 4, 2) * 8 + lax.rem(x + lax.rem(d, 4), 4) * 2

    barrier = pltpu.get_barrier_semaphore()
    pl.semaphore_signal(barrier, inc=1, device_id=(chan, sibling), device_id_type=MESH)
    for d in range(1, 8):
        pl.semaphore_signal(barrier, inc=1, device_id=(chan, place(d) + core), device_id_type=MESH)
    pl.semaphore_wait(barrier, 8)

    src32[...] = src_ref[...].astype(jnp.float32)

    def block(dest):
        total = None
        for w in range(wins):
            for i in range(per):
                s = dest * per + i
                first = src32[pl.ds(s, 1), 2 * w * freqs : (2 * w + 1) * freqs]
                second = src32[pl.ds(s, 1), (2 * w + 1) * freqs : (2 * w + 2) * freqs]
                cos, sin = cos_ref[...], sin_ref[...]
                mixed[w, i * LAGS : (i + 1) * LAGS, :freqs] = (first * cos + second * sin).astype(jnp.bfloat16)
                mixed[w, i * LAGS : (i + 1) * LAGS, freqs:] = (second * cos - first * sin).astype(jnp.bfloat16)
            term = lax.dot_general(
                mixed[w], rec_ref[:, 2 * w * freqs : (2 * w + 2) * freqs],
                (((1,), (1,)), ((), ())), preferred_element_type=jnp.float32,
            )
            total = term if total is None else total + term
        return total

    def copy1(d):
        return pltpu.make_async_remote_copy(
            src_ref=send1.at[d], dst_ref=recv1.at[d], send_sem=sem_s1.at[d], recv_sem=sem_r1.at[d],
            device_id=(chan, sibling), device_id_type=MESH,
        )

    def copy2(d):
        return pltpu.make_async_remote_copy(
            src_ref=send2.at[d], dst_ref=recv2.at[d], send_sem=sem_s2.at[d], recv_sem=sem_r2.at[d],
            device_id=(chan, place(d) + core), device_id_type=MESH,
        )

    @pl.loop(0, 8)
    def _(n):
        d = 7 - n
        send1[d] = block(place(d) + 1 - core).astype(jnp.bfloat16)
        copy1(d).start()

    @pl.loop(0, 7)
    def _(n):
        d = 7 - n
        part = block(place(d) + core)
        copy1(d).wait_recv()
        send2[d] = (part + recv1[d].astype(jnp.float32)).astype(jnp.bfloat16)
        copy2(d).start()

    total = block(win)
    copy1(0).wait_recv()
    total = total + recv1[0].astype(jnp.float32)
    for d in range(1, 8):
        copy2(d).wait_recv()
        total = total + recv2[d].astype(jnp.float32)
    out_ref[...] = (total * scale).astype(out_ref.dtype)
    for d in range(8):
        copy1(d).wait_send()
    for d in range(1, 8):
        copy2(d).wait_send()


def correlate(sources, receivers, cos, sin, scale):
    count, width = receivers.shape
    rows = SRC // 16 * LAGS
    blocks = pltpu.VMEM((8, rows, count), jnp.bfloat16)
    whole = pl.BlockSpec(memory_space=pltpu.VMEM)
    return pl.pallas_call(
        functools.partial(correlate_kernel, scale),
        out_shape=jax.ShapeDtypeStruct((rows, count), jnp.bfloat16),
        in_specs=[whole] * 4,
        out_specs=whole,
        scratch_shapes=[
            pltpu.VMEM((SRC, width), jnp.float32),
            pltpu.VMEM((width // (2 * cos.shape[1]), rows, 2 * cos.shape[1]), jnp.bfloat16),
            blocks, blocks, blocks, blocks,
            pltpu.SemaphoreType.DMA((8,)), pltpu.SemaphoreType.DMA((8,)),
            pltpu.SemaphoreType.DMA((8,)), pltpu.SemaphoreType.DMA((8,)),
        ],
        compiler_params=pltpu.CompilerParams(
            collective_id=0, has_side_effects=True, vmem_limit_bytes=32 * 1024 * 1024
        ),
        cost_estimate=pl.CostEstimate(
            flops=2 * SRC * LAGS * count * width, bytes_accessed=4 * count * width, transcendentals=0
        ),
        name="correlate",
    )(sources, receivers, cos, sin)


def exchange(values, flags, size):
    branches = [
        functools.partial(lax.ppermute, axis_name="chan", perm=[(i, i ^ t) for i in range(size)])
        for t in range(1, size)
    ]
    return lax.switch(flags - 1, branches, values)


def body(spectra, counts, partner):
    white = whiten_rows(spectra, counts[0])
    cos, sin = lag_table(spectra.shape[3], LAGS)
    size = lax.axis_size("chan")
    windows = spectra.shape[0] * lax.axis_size("win")
    flags = partner[0, 0]
    sources = exchange(white[:SRC], flags, size)
    block = correlate(sources, white, cos, sin, 1.0 / math.sqrt(windows))
    block = exchange(block, flags, size)
    out = jnp.swapaxes(block.astype(jnp.float32).reshape(SRC // 16, LAGS, white.shape[0]), 0, 1)
    return out[None, None]


def solution(mesh):
    return jax.shard_map(
        body,
        mesh=mesh,
        in_specs=(P("win", "chan", None, None), P("chan"), P()),
        out_specs=P("chan", None, None, "win", None),
        check_vma=False,
    )
```

```python
import functools
import math

import jax
import jax.numpy as jnp
from jax import lax
from jax.experimental import pallas as pl
from jax.experimental.pallas import tpu as pltpu
from jax.sharding import PartitionSpec as P

LAGS = 16
SRC = 160
MESH = pl.DeviceIdType.MESH


def whiten_rows(spectra, count):
    values = spectra.astype(jnp.float32)
    wins, block_size, two, freqs = spectra.shape
    valid = (jnp.arange(block_size, dtype=jnp.int32) < count).astype(jnp.float32)
    freq = jnp.arange(freqs, dtype=jnp.float32)
    taper = 0.75 - 0.25 * jnp.cos(2.0 * math.pi * (freq + 0.5) / freqs)
    power = jnp.mean(values * values, axis=(2, 3))
    scale = valid[None, :] / jnp.sqrt(power + 1e-05)
    white = (values * taper * scale[:, :, None, None]).astype(jnp.bfloat16)
    return jnp.swapaxes(white, 0, 1).reshape(block_size, wins * two * freqs)


def lag_table(freqs, lags):
    freq = jnp.arange(freqs, dtype=jnp.float32) + freqs // 4
    delay = jnp.arange(lags, dtype=jnp.float32) - lags // 2
    phase = 2.0 * math.pi * freq[None, :] * delay[:, None] / (4.0 * freqs)
    norm = 1.0 / math.sqrt(2.0 * freqs)
    return jnp.cos(phase) * norm, -jnp.sin(phase) * norm


def correlate_kernel(
    scale, src_ref, rec_ref, cos_ref, sin_ref, out_ref,
    src32, mixed, send1, recv1, send2, recv2, sem_s1, sem_r1, sem_s2, sem_r2,
):
    chan = lax.axis_index("chan")
    win = lax.axis_index("win")
    y, x, core = win // 8, lax.rem(win // 2, 4), lax.rem(win, 2)
    sibling = win + 1 - 2 * core
    per = SRC // 16
    rows = per * LAGS
    freqs = cos_ref.shape[1]
    wins = src_ref.shape[1] // (2 * freqs)

    def place(d):
        return lax.rem(y + d // 4, 2) * 8 + lax.rem(x + lax.rem(d, 4), 4) * 2

    barrier = pltpu.get_barrier_semaphore()
    pl.semaphore_signal(barrier, inc=1, device_id=(chan, sibling), device_id_type=MESH)
    for d in range(1, 8):
        pl.semaphore_signal(barrier, inc=1, device_id=(chan, place(d) + core), device_id_type=MESH)
    pl.semaphore_wait(barrier, 8)

    src32[...] = src_ref[...].astype(jnp.float32)

    def block(dest):
        total = None
        for w in range(wins):
            for i in range(per):
                s = dest * per + i
                first = src32[pl.ds(s, 1), 2 * w * freqs : (2 * w + 1) * freqs]
                second = src32[pl.ds(s, 1), (2 * w + 1) * freqs : (2 * w + 2) * freqs]
                cos, sin = cos_ref[...], sin_ref[...]
                mixed[w, i * LAGS : (i + 1) * LAGS, :freqs] = (first * cos + second * sin).astype(jnp.bfloat16)
                mixed[w, i * LAGS : (i + 1) * LAGS, freqs:] = (second * cos - first * sin).astype(jnp.bfloat16)
            term = lax.dot_general(
                mixed[w], rec_ref[:, 2 * w * freqs : (2 * w + 2) * freqs],
                (((1,), (1,)), ((), ())), preferred_element_type=jnp.float32,
            )
            total = term if total is None else total + term
        return total

    def copy1(d):
        return pltpu.make_async_remote_copy(
            src_ref=send1.at[d], dst_ref=recv1.at[d], send_sem=sem_s1.at[d], recv_sem=sem_r1.at[d],
            device_id=(chan, sibling), device_id_type=MESH,
        )

    def copy2(d):
        return pltpu.make_async_remote_copy(
            src_ref=send2.at[d], dst_ref=recv2.at[d], send_sem=sem_s2.at[d], recv_sem=sem_r2.at[d],
            device_id=(chan, place(d) + core), device_id_type=MESH,
        )

    @pl.loop(0, 8)
    def _(n):
        d = 7 - n
        send1[d] = block(place(d) + 1 - core).astype(jnp.bfloat16)
        copy1(d).start()

    @pl.loop(0, 7)
    def _(n):
        d = 7 - n
        part = block(place(d) + core)
        copy1(d).wait_recv()
        send2[d] = (part + recv1[d].astype(jnp.float32)).astype(jnp.bfloat16)
        copy2(d).start()

    total = block(win)
    copy1(0).wait_recv()
    total = total + recv1[0].astype(jnp.float32)
    for d in range(1, 8):
        copy2(d).wait_recv()
        total = total + recv2[d].astype(jnp.float32)
    out_ref[...] = (total * scale).astype(out_ref.dtype)
    for d in range(8):
        copy1(d).wait_send()
    for d in range(1, 8):
        copy2(d).wait_send()


def correlate(sources, receivers, cos, sin, scale):
    count, width = receivers.shape
    rows = SRC // 16 * LAGS
    blocks = pltpu.VMEM((8, rows, count), jnp.bfloat16)
    whole = pl.BlockSpec(memory_space=pltpu.VMEM)
    return pl.pallas_call(
        functools.partial(correlate_kernel, scale),
        out_shape=jax.ShapeDtypeStruct((rows, count), jnp.bfloat16),
        in_specs=[whole] * 4,
        out_specs=whole,
        scratch_shapes=[
            pltpu.VMEM((SRC, width), jnp.float32),
            pltpu.VMEM((width // (2 * cos.shape[1]), rows, 2 * cos.shape[1]), jnp.bfloat16),
            blocks, blocks, blocks, blocks,
            pltpu.SemaphoreType.DMA((8,)), pltpu.SemaphoreType.DMA((8,)),
            pltpu.SemaphoreType.DMA((8,)), pltpu.SemaphoreType.DMA((8,)),
        ],
        compiler_params=pltpu.CompilerParams(
            collective_id=0, has_side_effects=True, vmem_limit_bytes=32 * 1024 * 1024
        ),
        cost_estimate=pl.CostEstimate(
            flops=2 * SRC * LAGS * count * width, bytes_accessed=4 * count * width, transcendentals=0
        ),
        name="correlate",
    )(sources, receivers, cos, sin)


def flip(index, mask):
    for bit in range(mask.bit_length()):
        if (mask >> bit) & 1:
            index = index + (1 - 2 * lax.rem(index // (1 << bit), 2)) * (1 << bit)
    return index


def swap_kernel(mask, rows, src_ref, dst_ref, sem_s, sem_r):
    target = (flip(lax.axis_index("chan"), mask), lax.axis_index("win"))
    barrier = pltpu.get_barrier_semaphore()
    pl.semaphore_signal(barrier, inc=1, device_id=target, device_id_type=MESH)
    pl.semaphore_wait(barrier, 1)
    copies = [
        pltpu.make_async_remote_copy(
            src_ref=src_ref.at[pl.ds(n * rows, rows)], dst_ref=dst_ref.at[pl.ds(n * rows, rows)],
            send_sem=sem_s.at[n], recv_sem=sem_r.at[n], device_id=target, device_id_type=MESH,
        )
        for n in range(src_ref.shape[0] // rows)
    ]
    for copy in copies:
        copy.start()
    for copy in copies:
        copy.wait()


def swap(mask, rows, values):
    parts = values.shape[0] // rows
    return pl.pallas_call(
        functools.partial(swap_kernel, mask, rows),
        out_shape=jax.ShapeDtypeStruct(values.shape, values.dtype),
        in_specs=[pl.BlockSpec(memory_space=pl.ANY)],
        out_specs=pl.BlockSpec(memory_space=pl.ANY),
        scratch_shapes=[pltpu.SemaphoreType.DMA((parts,)), pltpu.SemaphoreType.DMA((parts,))],
        compiler_params=pltpu.CompilerParams(collective_id=mask, has_side_effects=True),
        name="swap",
    )(values)


def exchange(values, flags, size):
    branches = [functools.partial(swap, t, 32) for t in range(1, size)]
    return lax.switch(flags - 1, branches, values)


def send_back(values, flags, size):
    branches = [
        functools.partial(lax.ppermute, axis_name="chan", perm=[(i, i ^ t) for i in range(size)])
        for t in range(1, size)
    ]
    return lax.switch(flags - 1, branches, values)


def body(spectra, counts, partner):
    white = whiten_rows(spectra, counts[0])
    cos, sin = lag_table(spectra.shape[3], LAGS)
    size = lax.axis_size("chan")
    windows = spectra.shape[0] * lax.axis_size("win")
    flags = partner[0, 0]
    sources = exchange(white[:SRC], flags, size)
    block = correlate(sources, white, cos, sin, 1.0 / math.sqrt(windows))
    block = send_back(block, flags, size)
    out = jnp.swapaxes(block.astype(jnp.float32).reshape(SRC // 16, LAGS, white.shape[0]), 0, 1)
    return out[None, None]


def solution(mesh):
    return jax.shard_map(
        body,
        mesh=mesh,
        in_specs=(P("win", "chan", None, None), P("chan"), P()),
        out_specs=P("chan", None, None, "win", None),
        check_vma=False,
    )
```

```python
import functools
import math

import jax
import jax.numpy as jnp
import numpy as np
from jax import lax
from jax.experimental import pallas as pl
from jax.experimental.pallas import tpu as pltpu
from jax.sharding import PartitionSpec as P

LAGS = 16
SRC = 160
WIN = 16
PER = SRC // WIN
GROUP = 1
UNITS = PER // GROUP
STRIP = 32
DEPTH = 256
AHEAD = 3
MESH = pl.DeviceIdType.MESH


def lag_table(freqs):
    freq = np.arange(freqs, dtype=np.float64) + freqs // 4
    delay = np.arange(LAGS, dtype=np.float64) - LAGS // 2
    phase = 2.0 * np.pi * freq[None, :] * delay[:, None] / (4.0 * freqs)
    norm = 1.0 / math.sqrt(2.0 * freqs)
    return np.float32(np.cos(phase) * norm), np.float32(-np.sin(phase) * norm)


def taper_row(freqs):
    freq = np.arange(freqs, dtype=np.float64)
    taper = 0.75 - 0.25 * np.cos(2.0 * np.pi * (freq + 0.5) / freqs)
    return np.float32(np.concatenate([taper, taper])[None])


def flip(index, mask):
    for bit in range(mask.bit_length()):
        if (mask >> bit) & 1:
            index = index + (1 - 2 * lax.rem(index // (1 << bit), 2)) * (1 << bit)
    return index


def kernel(
    mask, scale, raw_ref, count_ref, taper_ref, cos_ref, sin_ref, out_ref,
    white, mine, theirs, rec_t, unit32, mixed, sums, part, own, send1, recv1, send2, recv2, back, landed,
    sem_xs, sem_xr, sem_1s, sem_1r, sem_2s, sem_2r, sem_bs, sem_br,
):
    chan, win = lax.axis_index("chan"), lax.axis_index("win")
    y, x, core = win // 8, lax.rem(win // 2, 4), lax.rem(win, 2)
    sibling = win + 1 - 2 * core
    partner = flip(chan, mask)
    freqs = cos_ref.shape[1]
    width = 2 * freqs
    count, total_width = raw_ref.shape
    wins = total_width // width
    rows = GROUP * LAGS

    def place(d):
        return lax.rem(y + d // 4, 2) * 8 + lax.rem(x + lax.rem(d, 4), 4) * 2

    barrier = pltpu.get_barrier_semaphore()
    pl.semaphore_signal(barrier, inc=1, device_id=(partner, win), device_id_type=MESH)
    pl.semaphore_signal(barrier, inc=1, device_id=(chan, sibling), device_id_type=MESH)

    @pl.loop(1, 8)
    def _(d):
        pl.semaphore_signal(barrier, inc=1, device_id=(chan, place(d) + core), device_id_type=MESH)

    def copy_x(unit):
        return pltpu.make_async_remote_copy(
            src_ref=mine.at[unit], dst_ref=theirs.at[unit], send_sem=sem_xs.at[unit], recv_sem=sem_xr.at[unit],
            device_id=(partner, win), device_id_type=MESH,
        )

    def copy_1(unit):
        return pltpu.make_async_remote_copy(
            src_ref=send1.at[unit], dst_ref=recv1.at[unit], send_sem=sem_1s.at[unit], recv_sem=sem_1r.at[unit],
            device_id=(chan, sibling), device_id_type=MESH,
        )

    def copy_2(unit, d, count=1):
        return pltpu.make_async_remote_copy(
            src_ref=send2.at[unit, pl.ds(d, count)], dst_ref=recv2.at[unit, pl.ds(d, count)],
            send_sem=sem_2s.at[unit], recv_sem=sem_2r.at[unit],
            device_id=(chan, place(d) + core), device_id_type=MESH,
        )

    def copy_b(unit):
        return pltpu.make_async_remote_copy(
            src_ref=back.at[unit], dst_ref=landed.at[unit], send_sem=sem_bs.at[unit], recv_sem=sem_br.at[unit],
            device_id=(partner, win), device_id_type=MESH,
        )

    def whiten(first, last):
        @pl.loop(first // STRIP, last // STRIP)
        def _(strip):
            at = pl.ds(pl.multiple_of(strip * STRIP, STRIP), STRIP)
            channel = strip * STRIP + lax.broadcasted_iota(jnp.int32, (STRIP, 1), 0)
            valid = jnp.where(channel < count_ref[...], 1.0, 0.0)
            for w in range(wins):
                piece = slice(w * width, (w + 1) * width)
                values = raw_ref[at, piece].astype(jnp.float32)
                power = jnp.sum(values * values, axis=1, keepdims=True) * (1.0 / width)
                values = values * taper_ref[...] * (valid / jnp.sqrt(power + 1e-05))
                for n in range(width // 128):
                    white[w * (width // 128) + n, at, :] = values[:, n * 128 : (n + 1) * 128]

    whiten(0, SRC)
    pl.semaphore_wait(barrier, 9)

    @pl.loop(0, UNITS)
    def _(unit):
        for i in range(GROUP):
            for n in range(total_width // 128):
                chosen = white[n, pl.ds(unit * GROUP + i, WIN, stride=PER), :]
                mine[unit, i * WIN : (i + 1) * WIN, n * 128 : (n + 1) * 128] = chosen.astype(jnp.bfloat16)

        @pl.when(unit < AHEAD)
        def _():
            copy_x(unit).start()

    whiten(SRC, count)

    @pl.loop(0, total_width // 128)
    def _(n):
        at = pl.ds(pl.multiple_of(n * 128, 128), 128)
        rec_t[at, :] = white[n].T.astype(jnp.bfloat16)

    def terms(unit):
        copy_x(unit).wait_recv()

        @pl.when(unit < UNITS - AHEAD)
        def _():
            copy_x(unit + AHEAD).start()

        unit32[...] = theirs[unit].astype(jnp.float32)

        @pl.loop(0, 16)
        def _(n):
            dest = place(lax.rem(n, 8)) + jnp.where(n < 8, 1 - core, core)
            cos, sin = cos_ref[...], sin_ref[...]
            for i in range(GROUP):
                source = i * WIN + dest
                into = pl.ds(pl.multiple_of(n * rows + i * LAGS, LAGS), LAGS)
                for w in range(wins):
                    a, b, c = w * width, w * width + freqs, (w + 1) * width
                    first, second = unit32[pl.ds(source, 1), a:b], unit32[pl.ds(source, 1), b:c]
                    mixed[into, a:b] = (first * cos + second * sin).astype(jnp.bfloat16)
                    mixed[into, b:c] = (second * cos - first * sin).astype(jnp.bfloat16)

        sums[...] = jnp.zeros_like(sums)

        @pl.loop(0, total_width // DEPTH)
        def _(n):
            at = pl.ds(pl.multiple_of(n * DEPTH, DEPTH), DEPTH)
            sums[...] += jnp.dot(mixed[:, at], rec_t[at, :], preferred_element_type=jnp.float32)

        send1[unit] = sums[: 8 * rows].astype(jnp.bfloat16).reshape(8, rows, count)
        copy_1(unit).start()
        part[lax.rem(unit, 2)] = sums[8 * rows :].reshape(8, rows, count)

    def pair_sums(unit):
        copy_1(unit).wait_recv()
        total = part[lax.rem(unit, 2)] + recv1[unit].astype(jnp.float32)
        own[lax.rem(unit, 2)] = total[0]
        send2[unit] = total.astype(jnp.bfloat16)

        @pl.loop(1, 8)
        def _(d):
            copy_2(unit, d).start()

    def all_sums(unit):
        copy_2(unit, 1, 7).wait_recv()
        total = own[lax.rem(unit, 2)]
        for d in range(1, 8):
            total = total + recv2[unit, d].astype(jnp.float32)
        back[unit] = (total * scale).astype(jnp.bfloat16)
        copy_b(unit).start()

    @pl.loop(0, UNITS + 2)
    def _(unit):
        @pl.when(unit < UNITS)
        def _():
            terms(unit)

        @pl.when((unit >= 1) & (unit < UNITS + 1))
        def _():
            pair_sums(unit - 1)

        @pl.when(unit >= 2)
        def _():
            all_sums(unit - 2)

    @pl.loop(0, UNITS)
    def _(unit):
        copy_x(unit).wait_send()
        copy_1(unit).wait_send()
        copy_2(unit, 1, 7).wait_send()
        copy_b(unit).wait_send()
        copy_b(unit).wait_recv()
        out_ref[unit] = landed[unit]


def correlate(mask, scale, raw, count, taper, cos, sin):
    channels, width = raw.shape
    rows = GROUP * LAGS
    blocks = pltpu.VMEM((UNITS, 8, rows, channels), jnp.bfloat16)
    units = pltpu.VMEM((UNITS, WIN * GROUP, width), jnp.bfloat16)
    results = pltpu.VMEM((UNITS, rows, channels), jnp.bfloat16)
    whole = pl.BlockSpec(memory_space=pltpu.VMEM)
    each = pltpu.SemaphoreType.DMA((UNITS,))
    return pl.pallas_call(
        functools.partial(kernel, mask, scale),
        out_shape=jax.ShapeDtypeStruct((UNITS, rows, channels), jnp.bfloat16),
        in_specs=[whole] * 5,
        out_specs=whole,
        scratch_shapes=[
            pltpu.VMEM((width // 128, channels, 128), jnp.float32),
            units, units,
            pltpu.VMEM((width, channels), jnp.bfloat16),
            pltpu.VMEM((WIN * GROUP, width), jnp.float32),
            pltpu.VMEM((16 * rows, width), jnp.bfloat16),
            pltpu.VMEM((16 * rows, channels), jnp.float32),
            pltpu.VMEM((2, 8, rows, channels), jnp.float32),
            pltpu.VMEM((2, rows, channels), jnp.float32),
            blocks, blocks, blocks, blocks, results, results,
            each, each, each, each, each, each, each, each,
        ],
        compiler_params=pltpu.CompilerParams(
            collective_id=mask, has_side_effects=True, vmem_limit_bytes=32 * 1024 * 1024
        ),
        cost_estimate=pl.CostEstimate(
            flops=2 * SRC * LAGS * channels * width, bytes_accessed=4 * channels * width, transcendentals=0
        ),
        name="correlate",
    )(raw, count, taper, cos, sin)


def body(spectra, counts, partner):
    wins, channels, two, freqs = spectra.shape
    size = lax.axis_size("chan")
    scale = 1.0 / math.sqrt(wins * lax.axis_size("win"))
    raw = jnp.swapaxes(spectra, 0, 1).reshape(channels, wins * two * freqs)
    operands = (raw, counts.reshape(1, 1), taper_row(freqs), *lag_table(freqs))
    branches = [functools.partial(correlate, t, scale) for t in range(1, size)]
    block = lax.switch(partner[0, 0] - 1, branches, *operands)
    out = block.reshape(PER, LAGS, channels).astype(jnp.float32)
    return jnp.swapaxes(out, 0, 1)[None, None]


def solution(mesh):
    return jax.shard_map(
        body,
        mesh=mesh,
        in_specs=(P("win", "chan", None, None), P("chan"), P()),
        out_specs=P("chan", None, None, "win", None),
        check_vma=False,
    )
```
